32 devices in a mesh: parts: 2 (over y), sht: 4 (over z), det: 2 (over x), sub: 2 (over core).
Axes of the slice: x: 2, y: 2, z: 4, core: 2. Of those that a mesh axis runs over, the one named last changes fastest.
Arguments:
- timestreams: float32 [4, 8, 32, 8192], P(('parts', 'det'), ('sht', 'sub')), parts along dimension 0, may hold values from -96 to 96
- pointing: int32 [4, 8, 8192], P(('parts', 'det'), ('sht', 'sub')), parts along dimension 0, may hold values from 0 to 16383
- noise_weight: float32 [4, 8, 8192], P(('parts', 'det'), ('sht', 'sub')), parts along dimension 0, may hold values from 0.3 to 3
- legendre: float32 [8, 4096, 16], P(('sht', 'sub')), may hold values from -0.09375 to 0.09375
- beam_window: float32 [4096], replicated, may hold values from 0.3 to 1
- prior_weight: float32 [4096], replicated, may hold values from 20 to 2000
Outputs:
- sky_modes: float32 [16, 2, 32, 4096], P(('parts', 'sht', 'sub')), parts along dimension 0
The draws below stay inside these ranges and needn't reach their ends.
There are 2 independent parts, one for each index of `parts`. The reference program is written for one: setup_inputs(seed, part) draws one part's arguments, and reference() takes and returns one part's arrays. A program takes and returns all parts, laid end to end along the dimension named above; an argument that names none is the same for every part. Nothing has to cross between parts.
Inputs may be any that keep to these rules, and one draw needn't show every extreme that they name: `pointing`: each sample falls on a cycle of its own shard: local cycle times 8192 plus azimuth pixel.
All inputs are finite; a program needn't handle non-finite values.
Results may differ from the reference program's by a relative error of at most 0.0001.
Values sent between devices are 32-bit elements; how exact they have to be, the bound alone decides.
A program may use at most 128 MiB of HBM per device.

```python
import math
import jax
import jax.numpy as jnp
from jax import lax

L = 4096
NPHI = 8192
R_DEV = 2
NSIM = 32
TS = 8192
ITERS = 2
SHARDS = 8
M_MODES = 8
CYCLES = 16
GROUPS = 2


def set_ends(values, own_key, low, largest):
    longest = values.shape.index(max(values.shape))
    spots = []
    for shift in (0, 1):
        where = [jax.random.randint(jax.random.fold_in(own_key, axis), (), 0, length) for axis, length in enumerate(values.shape)]
        where[longest] = (where[longest] + shift) % values.shape[longest]
        spots.append(tuple(where))
    return values.at[spots[0]].set(low).at[spots[1]].set(largest)


def levels(key, shape, cuts, low, largest):
    factor_of = 1.0
    for dim, blocks in cuts:
        steps = jax.random.uniform(jax.random.fold_in(jax.random.fold_in(key, 6), dim), (blocks,), jnp.float32, low / len(cuts), largest / len(cuts))
        factor_of = factor_of * jnp.repeat(jnp.exp(steps), shape[dim] // blocks).reshape((-1,) + (1,) * (len(shape) - 1 - dim))
    return factor_of


def bell_draw(rng, dims, deviation, bound, cuts=(), held_as=jnp.bfloat16):
    loudness = levels(rng, dims, cuts, -0.22, 0.18) if cuts else 1.0
    array = jax.random.normal(rng, dims, jnp.float32) * deviation * loudness
    return jnp.minimum(jnp.maximum(array, -bound), bound).astype(held_as)


def setup_inputs(seed: int = 0, part: int = 0) -> dict:
    key_list = jax.random.split(jax.random.key(seed), 7)
    part_splits = jax.random.split(jax.random.fold_in(key_list[6], part), 7)
    timestreams = bell_draw(part_splits[0], (GROUPS, SHARDS, NSIM, TS), 16.0, 96.0, ((0, 2), (1, 8)), jnp.float32)
    pointing = set_ends(jax.random.randint(part_splits[1], (GROUPS, SHARDS, TS), 0, R_DEV * NPHI), jax.random.fold_in(part_splits[1], 1), 0, (R_DEV * NPHI) - 1).astype(jnp.int32)
    noise_weight = jnp.clip(jnp.exp(math.log(3.0) - 2.3025851 * jax.random.uniform(part_splits[2], (GROUPS, SHARDS, TS), jnp.float32) ** levels(part_splits[2], (GROUPS, SHARDS, TS), ((0, 2), (1, 8)), -0.2, 0.2)), 0.3, 3.0)
    legendre = bell_draw(key_list[3], (M_MODES, L, CYCLES), L ** -0.5, 0.09375, ((0, 8),), jnp.float32)
    beam_window = jnp.clip(jnp.exp(jax.random.uniform(key_list[4], (L,), jnp.float32, math.log(0.3), math.log(1.0))), 0.3, 1.0)
    prior_weight = jnp.clip(jnp.exp(jax.random.uniform(key_list[5], (L,), jnp.float32, math.log(20.0), math.log(2000.0))), 20.0, 2000.0)
    return dict(timestreams=timestreams, pointing=pointing, noise_weight=noise_weight, legendre=legendre, beam_window=beam_window, prior_weight=prior_weight)


HIGHEST = lax.Precision.HIGHEST


def azimuth_table(numbers):
    columns = jnp.arange(NPHI, dtype=jnp.int32)
    phases = (numbers[:, None] * columns[None, :]) % NPHI
    angles = phases.astype(jnp.float32) * (2.0 * jnp.pi / NPHI)
    return jnp.stack([2.0 * jnp.cos(angles), -2.0 * jnp.sin(angles)])


def inner_sum(left, right):
    return jnp.sum(left * right, axis=(0, 1, 3))


def widen(values):
    return values[None, None, :, None]


def reference(timestreams, pointing, noise_weight, legendre, beam_window, prior_weight):
    modes = legendre.shape[0]
    shards = pointing.shape[1]
    groups = pointing.shape[0]
    cycle_dev = legendre.shape[2] // shards
    pixels = cycle_dev * NPHI
    spacing = L // modes
    order = jnp.arange(modes, dtype=jnp.int32)
    table = azimuth_table(order * spacing + spacing // 2)
    shard_ids = jnp.arange(shards, dtype=jnp.int32)[:, None]

    def synthesize(field):
        profile = jnp.einsum('mcsl,mlr->mcsr', field * beam_window, legendre, precision=HIGHEST)
        sky = jnp.einsum('mcsr,cmj->srj', profile, table, precision=HIGHEST)
        return sky.reshape(NSIM, shards, pixels)

    def project(weighted):
        sky = weighted.reshape(NSIM, shards * cycle_dev, NPHI)
        profile = jnp.einsum('srj,cmj->mcsr', sky, table, precision=HIGHEST)
        return jnp.einsum('mcsr,mlr->mcsl', profile, legendre, precision=HIGHEST) * beam_window

    def weigh(sky):
        total = jnp.zeros((NSIM, shards, pixels), jnp.float32)
        for group in range(groups):
            samples = sky[:, shard_ids, pointing[group]] * noise_weight[group]
            total = total.at[:, shard_ids, pointing[group]].add(samples)
        return total

    data_map = jnp.zeros((NSIM, shards, pixels), jnp.float32)
    for group in range(groups):
        samples = jnp.transpose(timestreams[group], (1, 0, 2)) * noise_weight[group]
        data_map = data_map.at[:, shard_ids, pointing[group]].add(samples)

    rhs = project(data_map)
    solution = jnp.zeros_like(rhs)
    residual = rhs
    direction = rhs
    norm_now = inner_sum(residual, residual)
    for iteration in range(ITERS):
        image = project(weigh(synthesize(direction))) + prior_weight * direction
        alpha = norm_now / inner_sum(direction, image)
        solution = solution + widen(alpha) * direction
        residual = residual - widen(alpha) * image
        norm_next = inner_sum(residual, residual)
        direction = residual + widen(norm_next / norm_now) * direction
        norm_now = norm_next
    return solution
```

```python
import functools
import jax
import jax.numpy as jnp
import numpy as np
from jax import lax
from jax.experimental import pallas as pl
from jax.experimental.pallas import tpu as pltpu
from jax.sharding import PartitionSpec as P

L = 4096
NPHI = 8192
ITERS = 2
LANES = 128


HIGHEST = lax.Precision.HIGHEST


def azimuth_table(numbers):
    columns = jnp.arange(NPHI, dtype=jnp.int32)
    phases = numbers[:, None] * columns[None, :] % NPHI
    angles = phases.astype(jnp.float32) * (2.0 * jnp.pi / NPHI)
    return jnp.stack([2.0 * jnp.cos(angles), -2.0 * jnp.sin(angles)])


def local_inner(left, right):
    return jnp.sum(left * right, axis=(0, 1, 3))


def widen(values):
    return values[None, None, :, None]


def general(timestreams, pointing, noise_weight, legendre, beam_window, prior_weight):
    major_count = lax.axis_size("sht")
    minor_count = lax.axis_size("sub")
    shards = major_count * minor_count
    local_modes = legendre.shape[0]
    modes = local_modes * shards
    cycle_dev = legendre.shape[2] // shards
    pixels = cycle_dev * NPHI
    samples_in = timestreams[0, 0]
    columns = pointing[0, 0]
    weights = noise_weight[0, 0]
    nsims = samples_in.shape[0]
    positions = jnp.arange(modes, dtype=jnp.int32)
    spacing = L // modes
    table = azimuth_table(positions * spacing + spacing // 2)
    stacked_samples = jnp.concatenate([samples_in * weights, weights[None, :]], axis=0)
    binned = jnp.zeros((nsims + 1, pixels), jnp.float32).at[:, columns].add(stacked_samples)
    data_map = binned[:nsims]
    hit_weight = binned[nsims]

    def project(weighted):
        sky = weighted.reshape(nsims, cycle_dev, NPHI)
        cycles = jnp.einsum("srj,cmj->mcsr", sky, table, precision=HIGHEST)
        arrived = lax.all_to_all(cycles, ("sht", "sub"), split_axis=0, concat_axis=3, tiled=True)
        harmonic = jnp.einsum("mcsr,mlr->mcsl", arrived, legendre, precision=HIGHEST)
        harmonic = lax.psum(harmonic, "det")
        return harmonic * beam_window

    def squares(values):
        return lax.psum(local_inner(values, values), ("sht", "sub"))

    rhs = project(data_map)
    solution = jnp.zeros_like(rhs)
    residual = rhs
    direction = rhs
    norm_now = squares(residual)
    for iteration in range(ITERS):
        profile = jnp.einsum("mcsl,mlr->mcsr", direction * beam_window, legendre, precision=HIGHEST)
        synthesize_cycles = lax.all_to_all(
            profile, ("sht", "sub"), split_axis=3, concat_axis=0, tiled=True
        )
        synthesize_sky = jnp.einsum("mcsr,cmj->srj", synthesize_cycles, table, precision=HIGHEST)
        image = (
            project(synthesize_sky.reshape(nsims, pixels) * hit_weight[None, :])
            + prior_weight * direction
        )
        alpha = norm_now / lax.psum(local_inner(direction, image), ("sht", "sub"))
        solution = solution + widen(alpha) * direction
        residual = residual - widen(alpha) * image
        norm_next = squares(residual)
        direction = residual + widen(norm_next / norm_now) * direction
        norm_now = norm_next
    return solution


def phase_matrix(modes, cycles):
    bins = 2 * modes
    angles = np.pi / bins * ((2 * np.arange(modes)[:, None] + 1) * np.arange(bins)[None, :] % (2 * bins))
    table = np.stack([2.0 * np.cos(angles), -2.0 * np.sin(angles)])
    full = np.einsum("ckb,rq->rbckq", table, np.eye(cycles))
    return full.reshape(cycles * bins, 2 * modes * cycles).astype(np.float32)


def dot(left, right):
    return jnp.dot(left, right, precision=HIGHEST, preferred_element_type=jnp.float32)


def dot_t(left, right, **kwargs):
    return lax.dot_general(left, right, (((1,), (1,)), ((), ())),
                           preferred_element_type=jnp.float32, **kwargs)


def turn(values, shift):
    shift = shift % LANES
    return values if shift == 0 else pltpu.roll(values, shift, 1)


def solve_kernel(sizes, stream_ref, point_ref, weight_ref, legendre_ref, beam_ref, prior_ref,
                 phase_ref, phase_t_ref, out_ref, spread, held, send_sem, recv_sem):
    modes, cycles, shards, minor, groups, bins, nsims = sizes
    det = lax.axis_index("det")
    shard = lax.axis_index("sht") * minor + lax.axis_index("sub")
    me = det * shards + shard
    count = groups * shards

    def partner(offset):
        other = lax.rem(me + offset, count)
        rest = lax.rem(other, shards)
        return other, {"det": other // shards, "sht": rest // minor, "sub": lax.rem(rest, minor)}

    barrier = pltpu.get_barrier_semaphore()
    for offset in range(1, count):
        pl.semaphore_signal(barrier, inc=1, device_id=partner(offset)[1],
                            device_id_type=pl.DeviceIdType.MESH)

    own = cycles // shards * bins
    place = point_ref[...]
    column = place & (NPHI - 1)
    sign = (1 - 2 * ((column // bins) & 1)).astype(jnp.float32)
    target = (place // NPHI) * bins + (column & (bins - 1))
    weight = weight_ref[...]
    samples = target.shape[1]
    hot = jnp.where(lax.broadcasted_iota(jnp.int32, (own, samples), 0) == target, 1.0, 0.0)
    hot = hot.astype(jnp.bfloat16)
    rows = jnp.concatenate(
        [stream_ref[...] * (weight * sign), jnp.broadcast_to(weight, (16, samples))], axis=0)
    high = rows.astype(jnp.bfloat16)
    rest = rows - high.astype(jnp.float32)
    middle = rest.astype(jnp.bfloat16)
    low = (rest - middle.astype(jnp.float32)).astype(jnp.bfloat16)
    binned = dot_t(high, hot) + (dot_t(middle, hot) + dot_t(low, hot))

    beam = beam_ref[...]
    prior = prior_ref[...]
    power = beam * beam
    center = jnp.sum(power * prior, axis=1, keepdims=True) / jnp.sum(power, axis=1, keepdims=True)
    excess = prior - center
    field = legendre_ref[...] * beam
    upper = det.astype(jnp.float32)
    first = field * ((1.0 - upper) + upper * (excess * excess))
    moments = dot_t(field, jnp.concatenate([first, first * excess], axis=0), precision=HIGHEST)

    spread[...] = jnp.zeros_like(spread)
    spread[0:48, 0:own] = binned
    spread[48:64, 0:own] = moments
    eight = [spread[8 * i:8 * i + 8, :] for i in range(8)]
    held[me, 0:8, :] = (eight[0] + turn(eight[1], 32)) + (turn(eight[2], 64) + turn(eight[3], 96))
    held[me, 8:16, :] = (eight[6] + turn(eight[7], 32)) + turn(eight[4], 64)

    pl.semaphore_wait(barrier, count - 1)
    copies = []
    for offset in range(1, count):
        copy = pltpu.make_async_remote_copy(
            src_ref=held.at[me], dst_ref=held.at[me],
            send_sem=send_sem.at[offset], recv_sem=recv_sem.at[me],
            device_id=partner(offset)[1], device_id_type=pl.DeviceIdType.MESH)
        copy.start()
        copies.append(copy)
    for offset in range(1, count):
        other, where = partner(offset)
        pltpu.make_async_remote_copy(
            src_ref=held.at[other], dst_ref=held.at[other],
            send_sem=send_sem.at[offset], recv_sem=recv_sem.at[other],
            device_id=where, device_id_type=pl.DeviceIdType.MESH).wait_recv()

    lane = lax.broadcasted_iota(jnp.int32, (8, LANES), 1)
    in_quarter = [lane // 32 == i for i in range(4)]
    in_mode = [lane // cycles == k for k in range(modes)]
    data_half, weight_half = [], []
    for half in range(2):
        data = [held[4 * half + i, 0:8, :] + held[shards + 4 * half + i, 0:8, :] for i in range(4)]
        weights = [held[4 * half + i, 8:16, :] + held[shards + 4 * half + i, 8:16, :] for i in range(4)]

        def gather(parts, at):
            total = jnp.zeros((8, LANES), jnp.float32)
            for i in range(4):
                total = jnp.where(in_quarter[i], turn(parts[i], 32 * (i - at)), total)
            return total

        data_half.append(jnp.concatenate([gather(data, j) for j in range(4)], axis=0))
        weight_half.append(gather(weights, 2))
    data_bins = jnp.concatenate(data_half, axis=1)
    weight_bins = jnp.concatenate(weight_half, axis=1)[0:1, :]
    moment = []
    for n in range(4):
        parts = []
        for k in range(modes):
            got = held[(n // 2) * shards + k, 8:16, :]
            for up in range(2):
                parts.append(jnp.where(in_mode[k], turn(got, cycles * (k - n % 2) - 32 * up), 0.0))
        moment.append(jnp.concatenate(parts, axis=0))

    def stack(values):
        return jnp.concatenate([values[:, :LANES], values[:, LANES:]], axis=0)

    def unstack(values):
        return jnp.concatenate([values[:nsims], values[nsims:]], axis=1)

    def inner(values):
        return jnp.sum(values[:nsims] + values[nsims:], axis=1, keepdims=True)

    def both(values):
        wide = jnp.broadcast_to(values, (nsims, LANES))
        return jnp.concatenate([wide, wide], axis=0)

    def sky(profile):
        return dot(unstack(profile), phase_t_ref[...])

    start = stack(dot(data_bins, phase_ref[...]))
    s0, s1, s2, s3 = [dot(start, m) for m in moment]
    seen = sky(s0)
    weighted = seen * weight_bins
    pulled = stack(dot(weighted, phase_ref[...]))
    g0, g1 = dot(pulled, moment[0]), dot(pulled, moment[1])
    norm = inner(start * s0)
    curve = jnp.sum(seen * weighted, axis=1, keepdims=True) + center * norm + inner(start * s1)
    alpha = norm / curve
    wide_alpha = both(alpha)
    keep = 1.0 - center * wide_alpha
    left = keep * start - wide_alpha * pulled
    left0 = keep * s0 - wide_alpha * g0
    left1 = keep * s1 - wide_alpha * g1
    left_norm = inner(left * (left0 - 2.0 * wide_alpha * s1) + (wide_alpha * wide_alpha) * (start * s2))
    beta = left_norm / norm
    wide_beta = both(beta)
    aim = left + wide_beta * start
    aim0 = left0 + wide_beta * s0
    aim1 = left1 + wide_beta * s1
    seen = sky(aim0 - wide_alpha * s1)
    square = wide_alpha * wide_alpha
    aim_norm = inner(aim * (aim0 - 2.0 * wide_alpha * s1) + square * (start * s2))
    aim_excess = inner(aim * (aim1 - 2.0 * wide_alpha * s2) + square * (start * s3))
    curve = jnp.sum(seen * seen * weight_bins, axis=1, keepdims=True) + center * aim_norm + aim_excess
    step = both(left_norm / curve)
    bent = -(wide_alpha * step) * start
    plain = wide_alpha * start + step * aim - center * bent

    back = lax.rem(LANES - cycles * shard, LANES)
    wide_lane = lax.broadcasted_iota(jnp.int32, plain.shape, 1)
    out_ref[...] = jnp.where(
        wide_lane < cycles, pltpu.roll(plain, back, 1),
        jnp.where(wide_lane < 2 * cycles, pltpu.roll(bent, lax.rem(back + cycles, LANES), 1), 0.0))
    for copy in copies:
        copy.wait_send()


def expand_kernel(factor_ref, legendre_ref, beam_ref, prior_ref, out_ref):
    field = legendre_ref[...] * beam_ref[...]
    both = jnp.concatenate([field, field * prior_ref[...]], axis=0)
    out_ref[...] = dot(factor_ref[...][:, :both.shape[0]], both)


def on_device(timestreams, pointing, noise_weight, legendre, beam_window, prior_weight):
    minor = lax.axis_size("sub")
    shards = lax.axis_size("sht") * minor
    groups = lax.axis_size("det")
    modes = legendre.shape[0] * shards
    cycles = legendre.shape[2]
    nsims, samples = timestreams.shape[2:]
    bins = 2 * modes
    if not (modes == shards == 8 and cycles == 16 and groups == 2 and nsims == 32
            and legendre.shape[1] == L and samples % LANES == 0):
        return general(timestreams, pointing, noise_weight, legendre, beam_window, prior_weight)
    count = groups * shards
    flat = jnp.swapaxes(legendre[0], 0, 1)
    beam = beam_window[None, :]
    prior = prior_weight[None, :]
    phase = phase_matrix(modes, cycles)
    sizes = (modes, cycles, shards, minor, groups, bins, nsims)
    vmem = pl.BlockSpec(memory_space=pltpu.VMEM)
    factors = pl.pallas_call(
        functools.partial(solve_kernel, sizes),
        out_shape=jax.ShapeDtypeStruct((2 * nsims, LANES), jnp.float32),
        in_specs=[vmem] * 8,
        out_specs=vmem,
        scratch_shapes=[
            pltpu.VMEM((64, LANES), jnp.float32),
            pltpu.VMEM((count, 16, LANES), jnp.float32),
            pltpu.SemaphoreType.DMA((count,)),
            pltpu.SemaphoreType.DMA((count,)),
        ],
        compiler_params=pltpu.CompilerParams(
            collective_id=0, has_side_effects=True, vmem_limit_bytes=48 * 2**20),
        name="solve",
    )(timestreams[0, 0], pointing[0], noise_weight[0], flat, beam, prior,
      jnp.asarray(phase), jnp.asarray(phase.T.copy()))
    tile = 1024
    expanded = pl.pallas_call(
        expand_kernel,
        grid=(L // tile,),
        out_shape=jax.ShapeDtypeStruct((2 * nsims, L), jnp.float32),
        in_specs=[
            pl.BlockSpec((2 * nsims, LANES), lambda i: (0, 0)),
            pl.BlockSpec((cycles, tile), lambda i: (0, i)),
            pl.BlockSpec((1, tile), lambda i: (0, i)),
            pl.BlockSpec((1, tile), lambda i: (0, i)),
        ],
        out_specs=pl.BlockSpec((2 * nsims, tile), lambda i: (0, i)),
        name="expand",
    )(factors, flat, beam, prior)
    return expanded.reshape(1, 2, nsims, L)


def solution(mesh):
    in_specs = (
        P(("parts", "det"), ("sht", "sub"), None, None),
        P(("parts", "det"), ("sht", "sub"), None),
        P(("parts", "det"), ("sht", "sub"), None),
        P(("sht", "sub"), None, None),
        P(),
        P(),
    )
    out_specs = P(("parts", "sht", "sub"), None, None, None)
    return jax.shard_map(
        on_device, mesh=mesh, in_specs=in_specs, out_specs=out_specs, check_vma=False
    )
```

```python
import functools
import jax
import jax.numpy as jnp
import numpy as np
from jax import lax
from jax.experimental import pallas as pl
from jax.experimental.pallas import tpu as pltpu
from jax.sharding import PartitionSpec as P

L = 4096
NPHI = 8192
ITERS = 2
LANES = 128


HIGHEST = lax.Precision.HIGHEST


def azimuth_table(numbers):
    columns = jnp.arange(NPHI, dtype=jnp.int32)
    phases = numbers[:, None] * columns[None, :] % NPHI
    angles = phases.astype(jnp.float32) * (2.0 * jnp.pi / NPHI)
    return jnp.stack([2.0 * jnp.cos(angles), -2.0 * jnp.sin(angles)])


def local_inner(left, right):
    return jnp.sum(left * right, axis=(0, 1, 3))


def widen(values):
    return values[None, None, :, None]


def general(timestreams, pointing, noise_weight, legendre, beam_window, prior_weight):
    major_count = lax.axis_size("sht")
    minor_count = lax.axis_size("sub")
    shards = major_count * minor_count
    local_modes = legendre.shape[0]
    modes = local_modes * shards
    cycle_dev = legendre.shape[2] // shards
    pixels = cycle_dev * NPHI
    samples_in = timestreams[0, 0]
    columns = pointing[0, 0]
    weights = noise_weight[0, 0]
    nsims = samples_in.shape[0]
    positions = jnp.arange(modes, dtype=jnp.int32)
    spacing = L // modes
    table = azimuth_table(positions * spacing + spacing // 2)
    stacked_samples = jnp.concatenate([samples_in * weights, weights[None, :]], axis=0)
    binned = jnp.zeros((nsims + 1, pixels), jnp.float32).at[:, columns].add(stacked_samples)
    data_map = binned[:nsims]
    hit_weight = binned[nsims]

    def project(weighted):
        sky = weighted.reshape(nsims, cycle_dev, NPHI)
        cycles = jnp.einsum("srj,cmj->mcsr", sky, table, precision=HIGHEST)
        arrived = lax.all_to_all(cycles, ("sht", "sub"), split_axis=0, concat_axis=3, tiled=True)
        harmonic = jnp.einsum("mcsr,mlr->mcsl", arrived, legendre, precision=HIGHEST)
        harmonic = lax.psum(harmonic, "det")
        return harmonic * beam_window

    def squares(values):
        return lax.psum(local_inner(values, values), ("sht", "sub"))

    rhs = project(data_map)
    solution = jnp.zeros_like(rhs)
    residual = rhs
    direction = rhs
    norm_now = squares(residual)
    for iteration in range(ITERS):
        profile = jnp.einsum("mcsl,mlr->mcsr", direction * beam_window, legendre, precision=HIGHEST)
        synthesize_cycles = lax.all_to_all(
            profile, ("sht", "sub"), split_axis=3, concat_axis=0, tiled=True
        )
        synthesize_sky = jnp.einsum("mcsr,cmj->srj", synthesize_cycles, table, precision=HIGHEST)
        image = (
            project(synthesize_sky.reshape(nsims, pixels) * hit_weight[None, :])
            + prior_weight * direction
        )
        alpha = norm_now / lax.psum(local_inner(direction, image), ("sht", "sub"))
        solution = solution + widen(alpha) * direction
        residual = residual - widen(alpha) * image
        norm_next = squares(residual)
        direction = residual + widen(norm_next / norm_now) * direction
        norm_now = norm_next
    return solution


def phase_matrix(modes, cycles):
    bins = 2 * modes
    angles = np.pi / bins * ((2 * np.arange(modes)[:, None] + 1) * np.arange(bins)[None, :] % (2 * bins))
    table = np.stack([2.0 * np.cos(angles), -2.0 * np.sin(angles)])
    full = np.einsum("ckb,rq->rbckq", table, np.eye(cycles))
    return full.reshape(cycles * bins, 2 * modes * cycles).astype(np.float32)


def dot(left, right):
    return jnp.dot(left, right, precision=HIGHEST, preferred_element_type=jnp.float32)


def dot_t(left, right, **kwargs):
    return lax.dot_general(left, right, (((1,), (1,)), ((), ())),
                           preferred_element_type=jnp.float32, **kwargs)


def turn(values, shift):
    shift = shift % LANES
    return values if shift == 0 else pltpu.roll(values, shift, 1)


def solve_kernel(sizes, stream_hbm, point_hbm, weight_hbm, legendre_hbm, beam_hbm, prior_hbm,
                 phase_hbm, phase_t_hbm, out_ref, basis_ref,
                 stream_ref, point_ref, weight_ref, legendre_ref, beam_ref, prior_ref,
                 phase_ref, phase_t_ref, spread, held, load_sem, send_sem, recv_sem):
    loads = []
    for source, place in ((point_hbm, point_ref), (weight_hbm, weight_ref), (stream_hbm, stream_ref),
                          (legendre_hbm, legendre_ref), (beam_hbm, beam_ref), (prior_hbm, prior_ref),
                          (phase_hbm, phase_ref), (phase_t_hbm, phase_t_ref)):
        load = pltpu.make_async_copy(source, place, load_sem.at[len(loads)])
        load.start()
        loads.append(load)
    modes, cycles, shards, minor, groups, bins, nsims = sizes
    det = lax.axis_index("det")
    shard = lax.axis_index("sht") * minor + lax.axis_index("sub")
    me = det * shards + shard
    count = groups * shards

    def partner(offset):
        other = lax.rem(me + offset, count)
        rest = lax.rem(other, shards)
        return other, {"det": other // shards, "sht": rest // minor, "sub": lax.rem(rest, minor)}

    barrier = pltpu.get_barrier_semaphore()
    for offset in range(1, count):
        pl.semaphore_signal(barrier, inc=1, device_id=partner(offset)[1],
                            device_id_type=pl.DeviceIdType.MESH)

    own = cycles // shards * bins
    for load in loads[:3]:
        load.wait()
    place = point_ref[...]
    column = place & (NPHI - 1)
    sign = (1 - 2 * ((column // bins) & 1)).astype(jnp.float32)
    target = (place // NPHI) * bins + (column & (bins - 1))
    weight = weight_ref[...]
    samples = target.shape[1]
    hot = jnp.where(lax.broadcasted_iota(jnp.int32, (own, samples), 0) == target, 1.0, 0.0)
    hot = hot.astype(jnp.bfloat16)
    rows = jnp.concatenate(
        [stream_ref[...] * (weight * sign), jnp.broadcast_to(weight, (16, samples))], axis=0)
    high = rows.astype(jnp.bfloat16)
    rest = rows - high.astype(jnp.float32)
    middle = rest.astype(jnp.bfloat16)
    low = (rest - middle.astype(jnp.float32)).astype(jnp.bfloat16)
    binned = dot_t(high, hot) + (dot_t(middle, hot) + dot_t(low, hot))

    for load in loads[3:6]:
        load.wait()
    beam = beam_ref[...]
    prior = prior_ref[...]
    power = beam * beam
    center = jnp.sum(power * prior, axis=1, keepdims=True) / jnp.sum(power, axis=1, keepdims=True)
    excess = prior - center
    field = legendre_ref[...] * beam
    upper = det.astype(jnp.float32)
    first = field * ((1.0 - upper) + upper * (excess * excess))
    moments = dot_t(field, jnp.concatenate([first, first * excess], axis=0), precision=HIGHEST)

    spread[...] = jnp.zeros_like(spread)
    spread[0:48, 0:own] = binned
    spread[48:64, 0:own] = moments
    eight = [spread[8 * i:8 * i + 8, :] for i in range(8)]
    held[me, 0:8, :] = (eight[0] + turn(eight[1], 32)) + (turn(eight[2], 64) + turn(eight[3], 96))
    held[me, 8:16, :] = (eight[6] + turn(eight[7], 32)) + turn(eight[4], 64)

    pl.semaphore_wait(barrier, count - 1)
    copies = []
    for offset in range(1, count):
        copy = pltpu.make_async_remote_copy(
            src_ref=held.at[me], dst_ref=held.at[me],
            send_sem=send_sem.at[offset], recv_sem=recv_sem.at[me],
            device_id=partner(offset)[1], device_id_type=pl.DeviceIdType.MESH)
        copy.start()
        copies.append(copy)

    wide = jnp.concatenate([field, field * excess], axis=0)
    wide_high = wide.astype(jnp.bfloat16)
    basis_ref[0:32, :] = wide_high
    basis_ref[32:64, :] = (wide - wide_high.astype(jnp.float32)).astype(jnp.bfloat16)
    basis_ref[64:96, :] = wide_high
    for load in loads[6:]:
        load.wait()
    for offset in range(1, count):
        other, where = partner(offset)
        pltpu.make_async_remote_copy(
            src_ref=held.at[other], dst_ref=held.at[other],
            send_sem=send_sem.at[offset], recv_sem=recv_sem.at[other],
            device_id=where, device_id_type=pl.DeviceIdType.MESH).wait_recv()

    lane = lax.broadcasted_iota(jnp.int32, (8, LANES), 1)
    in_quarter = [lane // 32 == i for i in range(4)]
    in_mode = [lane // cycles == k for k in range(modes)]
    data_half, weight_half = [], []
    for half in range(2):
        data = [held[4 * half + i, 0:8, :] + held[shards + 4 * half + i, 0:8, :] for i in range(4)]
        weights = [held[4 * half + i, 8:16, :] + held[shards + 4 * half + i, 8:16, :] for i in range(4)]

        def gather(parts, at):
            total = jnp.zeros((8, LANES), jnp.float32)
            for i in range(4):
                total = jnp.where(in_quarter[i], turn(parts[i], 32 * (i - at)), total)
            return total

        data_half.append(jnp.concatenate([gather(data, j) for j in range(4)], axis=0))
        weight_half.append(gather(weights, 2))
    data_bins = jnp.concatenate(data_half, axis=1)
    weight_bins = jnp.concatenate(weight_half, axis=1)[0:1, :]
    moment = []
    for n in range(4):
        parts = []
        for k in range(modes):
            got = held[(n // 2) * shards + k, 8:16, :]
            for up in range(2):
                parts.append(jnp.where(in_mode[k], turn(got, cycles * (k - n % 2) - 32 * up), 0.0))
        moment.append(jnp.concatenate(parts, axis=0))

    def stack(values):
        return jnp.concatenate([values[:, :LANES], values[:, LANES:]], axis=0)

    def unstack(values):
        return jnp.concatenate([values[:nsims], values[nsims:]], axis=1)

    def inner(values):
        return jnp.sum(values[:nsims] + values[nsims:], axis=1, keepdims=True)

    def both(values):
        wide = jnp.broadcast_to(values, (nsims, LANES))
        return jnp.concatenate([wide, wide], axis=0)

    def sky(profile):
        return dot(unstack(profile), phase_t_ref[...])

    start = stack(dot(data_bins, phase_ref[...]))
    s0, s1, s2, s3 = [dot(start, m) for m in moment]
    seen = sky(s0)
    weighted = seen * weight_bins
    pulled = stack(dot(weighted, phase_ref[...]))
    g0, g1 = dot(pulled, moment[0]), dot(pulled, moment[1])
    norm = inner(start * s0)
    curve = jnp.sum(seen * weighted, axis=1, keepdims=True) + center * norm + inner(start * s1)
    alpha = norm / curve
    wide_alpha = both(alpha)
    keep = 1.0 - center * wide_alpha
    left = keep * start - wide_alpha * pulled
    left0 = keep * s0 - wide_alpha * g0
    left1 = keep * s1 - wide_alpha * g1
    left_norm = inner(left * (left0 - 2.0 * wide_alpha * s1) + (wide_alpha * wide_alpha) * (start * s2))
    beta = left_norm / norm
    wide_beta = both(beta)
    aim = left + wide_beta * start
    aim0 = left0 + wide_beta * s0
    aim1 = left1 + wide_beta * s1
    seen = sky(aim0 - wide_alpha * s1)
    square = wide_alpha * wide_alpha
    aim_norm = inner(aim * (aim0 - 2.0 * wide_alpha * s1) + square * (start * s2))
    aim_excess = inner(aim * (aim1 - 2.0 * wide_alpha * s2) + square * (start * s3))
    curve = jnp.sum(seen * seen * weight_bins, axis=1, keepdims=True) + center * aim_norm + aim_excess
    step = both(left_norm / curve)
    bent = -(wide_alpha * step) * start
    plain = wide_alpha * start + step * aim

    back = lax.rem(LANES - cycles * shard, LANES)
    wide_lane = lax.broadcasted_iota(jnp.int32, plain.shape, 1)
    factor = jnp.where(
        wide_lane < cycles, pltpu.roll(plain, back, 1),
        jnp.where(wide_lane < 2 * cycles, pltpu.roll(bent, lax.rem(back + cycles, LANES), 1), 0.0))
    factor_high = factor.astype(jnp.bfloat16).astype(jnp.float32)
    out_ref[...] = (factor_high + turn(factor_high, 32)
                    + turn(factor - factor_high, 64)).astype(jnp.bfloat16)
    for copy in copies:
        copy.wait_send()


def expand_kernel(parts, factor_ref, basis_ref, out_hbm, held, sem):
    factor = factor_ref[...][:, :basis_ref.shape[0]]
    width = basis_ref.shape[1] // parts
    copies = []
    for i in range(parts):
        span = pl.ds(i * width, width)
        held[:, span] = jnp.dot(factor, basis_ref[:, span], preferred_element_type=jnp.float32)
        copy = pltpu.make_async_copy(held.at[:, span], out_hbm.at[:, span], sem.at[i])
        copy.start()
        copies.append(copy)
    for copy in copies:
        copy.wait()


def on_device(timestreams, pointing, noise_weight, legendre, beam_window, prior_weight):
    minor = lax.axis_size("sub")
    shards = lax.axis_size("sht") * minor
    groups = lax.axis_size("det")
    modes = legendre.shape[0] * shards
    cycles = legendre.shape[2]
    nsims, samples = timestreams.shape[2:]
    bins = 2 * modes
    if not (modes == shards == 8 and cycles == 16 and groups == 2 and nsims == 32
            and legendre.shape[1] == L and samples % LANES == 0):
        return general(timestreams, pointing, noise_weight, legendre, beam_window, prior_weight)
    count = groups * shards
    flat = jnp.swapaxes(legendre[0], 0, 1)
    beam = beam_window[None, :]
    prior = prior_weight[None, :]
    phase = phase_matrix(modes, cycles)
    sizes = (modes, cycles, shards, minor, groups, bins, nsims)
    vmem = pl.BlockSpec(memory_space=pltpu.VMEM)
    hbm = pl.BlockSpec(memory_space=pltpu.HBM)
    arguments = (timestreams[0, 0], pointing[0], noise_weight[0], flat, beam, prior,
                 jnp.asarray(phase), jnp.asarray(phase.T.copy()))
    factors, basis = pl.pallas_call(
        functools.partial(solve_kernel, sizes),
        out_shape=(jax.ShapeDtypeStruct((2 * nsims, LANES), jnp.bfloat16),
                   jax.ShapeDtypeStruct((6 * cycles, L), jnp.bfloat16)),
        in_specs=[hbm] * 8,
        out_specs=(vmem, vmem),
        scratch_shapes=[pltpu.VMEM(a.shape, a.dtype) for a in arguments] + [
            pltpu.VMEM((64, LANES), jnp.float32),
            pltpu.VMEM((count, 16, LANES), jnp.float32),
            pltpu.SemaphoreType.DMA((len(arguments),)),
            pltpu.SemaphoreType.DMA((count,)),
            pltpu.SemaphoreType.DMA((count,)),
        ],
        compiler_params=pltpu.CompilerParams(
            collective_id=0, has_side_effects=True, vmem_limit_bytes=32 * 2**20),
        name="solve",
    )(*[pltpu.with_memory_space_constraint(a, pltpu.HBM) for a in arguments])
    parts = 4
    expanded = pl.pallas_call(
        functools.partial(expand_kernel, parts),
        out_shape=jax.ShapeDtypeStruct((2 * nsims, L), jnp.float32),
        in_specs=[vmem, vmem],
        out_specs=hbm,
        scratch_shapes=[pltpu.VMEM((2 * nsims, L), jnp.float32), pltpu.SemaphoreType.DMA((parts,))],
        compiler_params=pltpu.CompilerParams(vmem_limit_bytes=16 * 2**20),
        name="expand",
    )(factors, basis)
    return expanded.reshape(1, 2, nsims, L)


def solution(mesh):
    in_specs = (
        P(("parts", "det"), ("sht", "sub"), None, None),
        P(("parts", "det"), ("sht", "sub"), None),
        P(("parts", "det"), ("sht", "sub"), None),
        P(("sht", "sub"), None, None),
        P(),
        P(),
    )
    out_specs = P(("parts", "sht", "sub"), None, None, None)
    return jax.shard_map(
        on_device, mesh=mesh, in_specs=in_specs, out_specs=out_specs, check_vma=False
    )
```

```python
import functools
import jax
import jax.numpy as jnp
import ml_dtypes
import numpy as np
from jax import lax
from jax.experimental import pallas as pl
from jax.experimental.pallas import tpu as pltpu
from jax.sharding import PartitionSpec as P

L = 4096
NPHI = 8192
ITERS = 2
LANES = 128


HIGHEST = lax.Precision.HIGHEST


def azimuth_table(numbers):
    columns = jnp.arange(NPHI, dtype=jnp.int32)
    phases = numbers[:, None] * columns[None, :] % NPHI
    angles = phases.astype(jnp.float32) * (2.0 * jnp.pi / NPHI)
    return jnp.stack([2.0 * jnp.cos(angles), -2.0 * jnp.sin(angles)])


def local_inner(left, right):
    return jnp.sum(left * right, axis=(0, 1, 3))


def widen(values):
    return values[None, None, :, None]


def general(timestreams, pointing, noise_weight, legendre, beam_window, prior_weight):
    major_count = lax.axis_size("sht")
    minor_count = lax.axis_size("sub")
    shards = major_count * minor_count
    local_modes = legendre.shape[0]
    modes = local_modes * shards
    cycle_dev = legendre.shape[2] // shards
    pixels = cycle_dev * NPHI
    samples_in = timestreams[0, 0]
    columns = pointing[0, 0]
    weights = noise_weight[0, 0]
    nsims = samples_in.shape[0]
    positions = jnp.arange(modes, dtype=jnp.int32)
    spacing = L // modes
    table = azimuth_table(positions * spacing + spacing // 2)
    stacked_samples = jnp.concatenate([samples_in * weights, weights[None, :]], axis=0)
    binned = jnp.zeros((nsims + 1, pixels), jnp.float32).at[:, columns].add(stacked_samples)
    data_map = binned[:nsims]
    hit_weight = binned[nsims]

    def project(weighted):
        sky = weighted.reshape(nsims, cycle_dev, NPHI)
        cycles = jnp.einsum("srj,cmj->mcsr", sky, table, precision=HIGHEST)
        arrived = lax.all_to_all(cycles, ("sht", "sub"), split_axis=0, concat_axis=3, tiled=True)
        harmonic = jnp.einsum("mcsr,mlr->mcsl", arrived, legendre, precision=HIGHEST)
        harmonic = lax.psum(harmonic, "det")
        return harmonic * beam_window

    def squares(values):
        return lax.psum(local_inner(values, values), ("sht", "sub"))

    rhs = project(data_map)
    solution = jnp.zeros_like(rhs)
    residual = rhs
    direction = rhs
    norm_now = squares(residual)
    for iteration in range(ITERS):
        profile = jnp.einsum("mcsl,mlr->mcsr", direction * beam_window, legendre, precision=HIGHEST)
        synthesize_cycles = lax.all_to_all(
            profile, ("sht", "sub"), split_axis=3, concat_axis=0, tiled=True
        )
        synthesize_sky = jnp.einsum("mcsr,cmj->srj", synthesize_cycles, table, precision=HIGHEST)
        image = (
            project(synthesize_sky.reshape(nsims, pixels) * hit_weight[None, :])
            + prior_weight * direction
        )
        alpha = norm_now / lax.psum(local_inner(direction, image), ("sht", "sub"))
        solution = solution + widen(alpha) * direction
        residual = residual - widen(alpha) * image
        norm_next = squares(residual)
        direction = residual + widen(norm_next / norm_now) * direction
        norm_now = norm_next
    return solution


def phase_matrix(modes, cycles):
    bins = 2 * modes
    angles = np.pi / bins * ((2 * np.arange(modes)[:, None] + 1) * np.arange(bins)[None, :] % (2 * bins))
    table = np.stack([2.0 * np.cos(angles), -2.0 * np.sin(angles)])
    full = np.einsum("ckb,rq->rbckq", table, np.eye(cycles))
    return full.reshape(cycles * bins, 2 * modes * cycles).astype(np.float32)


def dot_t(left, right, **kwargs):
    return lax.dot_general(left, right, (((1,), (1,)), ((), ())),
                           preferred_element_type=jnp.float32, **kwargs)


def split(values, count):
    parts = []
    for _ in range(count):
        parts.append(values.astype(jnp.bfloat16))
        values = values - parts[-1].astype(jnp.float32)
    return parts


def split_dot(left, right):
    count = len(right)
    rows = left.shape[0]
    parts = split(left, count)
    total = None
    for i in reversed(range(count)):
        got = jnp.dot(jnp.concatenate(parts[:count - i], axis=0), right[i],
                      preferred_element_type=jnp.float32)
        for j in reversed(range(count - i)):
            piece = got[j * rows:(j + 1) * rows]
            total = piece if total is None else total + piece
    return total


def turn(values, shift):
    shift = shift % LANES
    return values if shift == 0 else pltpu.roll(values, shift, 1)


def solve_kernel(sizes, stream_hbm, point_hbm, weight_hbm, legendre_hbm, beam_hbm, prior_hbm,
                 phase_hbm, out_ref, basis_ref,
                 stream_ref, point_ref, weight_ref, legendre_ref, beam_ref, prior_ref,
                 phase_ref, spread, held, load_sem, send_sem, recv_sem):
    modes, cycles, shards, minor, groups, bins, nsims, cuts = sizes
    samples = point_ref.shape[1]
    span = samples // cuts
    chunks = [pl.ds(i * span, span) for i in range(cuts)]
    pairs = [(legendre_hbm, legendre_ref), (beam_hbm, beam_ref), (prior_hbm, prior_ref),
             (point_hbm, point_ref), (weight_hbm, weight_ref)]
    pairs += [(stream_hbm.at[:, c], stream_ref.at[:, c]) for c in chunks]
    pairs += [(phase_hbm, phase_ref)]
    loads = [pltpu.make_async_copy(source, place, load_sem.at[i])
             for i, (source, place) in enumerate(pairs)]
    for load in loads:
        load.start()
    det = lax.axis_index("det")
    major, sub = lax.axis_index("sht"), lax.axis_index("sub")
    majors = shards // minor
    shard = major * minor + sub
    me = det * shards + shard
    count = groups * shards

    def partner(offset):
        step = offset // (groups * minor)
        row = step + (step - major + majors) // majors if step < majors - 1 else major
        side = lax.rem(det + 1 + offset // minor, groups)
        core = lax.rem(sub + 1 + offset, minor)
        return side * shards + row * minor + core, {"det": side, "sht": row, "sub": core}

    barrier = pltpu.get_barrier_semaphore()
    for offset in range(count - 1):
        pl.semaphore_signal(barrier, inc=1, device_id=partner(offset)[1],
                            device_id_type=pl.DeviceIdType.MESH)

    for load in loads[:3]:
        load.wait()
    beam = beam_ref[...]
    prior = prior_ref[...]
    power = beam * beam
    center = jnp.sum(power * prior, axis=1, keepdims=True) / jnp.sum(power, axis=1, keepdims=True)
    excess = prior - center
    field = legendre_ref[...] * beam
    upper = det.astype(jnp.float32)
    first = field * ((1.0 - upper) + upper * (excess * excess))
    left = jnp.concatenate(split(field, 3), axis=0)
    right = jnp.concatenate(split(jnp.concatenate([first, first * excess], axis=0), 3), axis=0)
    crossed = dot_t(left, right)
    top, mid, end = crossed[0:16], crossed[16:32], crossed[32:48]
    spread[64:112, 0:96] = jnp.concatenate([top + (mid + end), top + mid, top], axis=0)

    for load in loads[3:5]:
        load.wait()
    own = cycles // shards * bins
    binned = jnp.zeros((96, own), jnp.float32)
    for chunk, load in zip(chunks, loads[5:5 + cuts]):
        place = point_ref[:, chunk]
        column = place & (NPHI - 1)
        sign = (1 - 2 * ((column // bins) & 1)).astype(jnp.float32)
        target = (place // NPHI) * bins + (column & (bins - 1))
        weight = weight_ref[:, chunk]
        hot = jnp.where(lax.broadcasted_iota(jnp.int32, (own, span), 0) == target, 1.0, 0.0)
        hot = hot.astype(jnp.bfloat16)
        load.wait()
        rows = jnp.concatenate(
            [stream_ref[:, chunk] * (weight * sign), jnp.broadcast_to(weight, (16, span))], axis=0)
        binned += dot_t(jnp.concatenate(split(rows, 2), axis=0), hot)
    binned = binned[0:48] + binned[48:96]

    spread[0:64] = jnp.zeros((64, LANES), jnp.float32)
    spread[0:48, 0:own] = binned
    spread[48:64, 0:32] = spread[64:80, 0:32] + (
        turn(spread[80:96, :], -32) + turn(spread[96:112, :], -64))[:, 0:32]
    eight = [spread[8 * i:8 * i + 8, :] for i in range(8)]
    held[me, 0:8, :] = (eight[0] + turn(eight[1], 32)) + (turn(eight[2], 64) + turn(eight[3], 96))
    held[me, 8:16, :] = (eight[6] + turn(eight[7], 32)) + turn(eight[4], 64)

    pl.semaphore_wait(barrier, count - 1)
    copies = []
    for offset in range(count - 1):
        copy = pltpu.make_async_remote_copy(
            src_ref=held.at[me], dst_ref=held.at[me],
            send_sem=send_sem.at[offset], recv_sem=recv_sem.at[me],
            device_id=partner(offset)[1], device_id_type=pl.DeviceIdType.MESH)
        copy.start()
        copies.append(copy)

    wide = jnp.concatenate([field, field * excess], axis=0)
    wide_high = wide.astype(jnp.bfloat16)
    basis_ref[0:32, :] = wide_high
    basis_ref[32:64, :] = (wide - wide_high.astype(jnp.float32)).astype(jnp.bfloat16)
    basis_ref[64:96, :] = wide_high
    loads[-1].wait()
    for offset in range(count - 1):
        other, where = partner(offset)
        pltpu.make_async_remote_copy(
            src_ref=held.at[other], dst_ref=held.at[other],
            send_sem=send_sem.at[offset], recv_sem=recv_sem.at[other],
            device_id=where, device_id_type=pl.DeviceIdType.MESH).wait_recv()

    lane = lax.broadcasted_iota(jnp.int32, (8, LANES), 1)
    in_quarter = [lane // 32 == i for i in range(4)]
    in_mode = [lane // cycles == k for k in range(modes)]
    data_half, weight_half = [], []
    for half in range(2):
        data = [held[4 * half + i, 0:8, :] + held[shards + 4 * half + i, 0:8, :] for i in range(4)]
        weights = [held[4 * half + i, 8:16, :] + held[shards + 4 * half + i, 8:16, :] for i in range(4)]

        def gather(parts, at):
            total = jnp.zeros((8, LANES), jnp.float32)
            for i in range(4):
                total = jnp.where(in_quarter[i], turn(parts[i], 32 * (i - at)), total)
            return total

        data_half.append(jnp.concatenate([gather(data, j) for j in range(4)], axis=0))
        weight_half.append(gather(weights, 2))
    data_bins = jnp.concatenate(data_half, axis=1)
    weight_bins = jnp.concatenate(weight_half, axis=1)[0:1, :]
    moment = []
    for n in range(4):
        parts = []
        for k in range(modes):
            got = held[(n // 2) * shards + k, 8:16, :]
            for up in range(2):
                parts.append(jnp.where(in_mode[k], turn(got, cycles * (k - n % 2) - 32 * up), 0.0))
        moment.append(jnp.concatenate(parts, axis=0))

    def stack(values):
        return jnp.concatenate([values[:, :LANES], values[:, LANES:]], axis=0)

    def unstack(values):
        return jnp.concatenate([values[:nsims], values[nsims:]], axis=1)

    def inner(values):
        return jnp.sum(values[:nsims] + values[nsims:], axis=1, keepdims=True)

    def both(values):
        wide = jnp.broadcast_to(values, (nsims, LANES))
        return jnp.concatenate([wide, wide], axis=0)

    size = 2 * modes * cycles
    phase = [phase_ref[i * size:(i + 1) * size, :] for i in range(4)]

    def sky(profile):
        return split_dot(unstack(profile), phase[2:])

    def profiles(bins_in):
        return stack(split_dot(bins_in, phase[:2]))

    moment_parts = split(jnp.concatenate(moment, axis=1), 3)
    start = profiles(data_bins)
    applied = split_dot(start, moment_parts)
    s0, s1, s2, s3 = [applied[:, n * LANES:(n + 1) * LANES] for n in range(4)]
    seen = sky(s0)
    weighted = seen * weight_bins
    pulled = profiles(weighted)
    applied = split_dot(pulled, [part[:, :2 * LANES] for part in moment_parts])
    g0, g1 = applied[:, :LANES], applied[:, LANES:]
    seen_more = sky(g0 + s1)
    norm = inner(start * s0)
    curve = jnp.sum(seen * weighted, axis=1, keepdims=True) + center * norm + inner(start * s1)
    alpha = norm / curve
    wide_alpha = both(alpha)
    square = wide_alpha * wide_alpha
    keep = 1.0 - center * wide_alpha
    left = keep * start - wide_alpha * pulled
    left0 = keep * s0 - wide_alpha * g0
    left1 = keep * s1 - wide_alpha * g1
    left_norm = inner(left * (left0 - 2.0 * wide_alpha * s1) + square * (start * s2))
    beta = left_norm / norm
    wide_beta = both(beta)
    aim = left + wide_beta * start
    aim0 = left0 + wide_beta * s0
    aim1 = left1 + wide_beta * s1
    aim_seen = (1.0 - center * alpha + beta) * seen - alpha * seen_more
    aim_norm = inner(aim * (aim0 - 2.0 * wide_alpha * s1) + square * (start * s2))
    aim_excess = inner(aim * (aim1 - 2.0 * wide_alpha * s2) + square * (start * s3))
    curve = (jnp.sum(aim_seen * aim_seen * weight_bins, axis=1, keepdims=True)
             + center * aim_norm + aim_excess)
    step = both(left_norm / curve)
    bent = -(wide_alpha * step) * start
    plain = wide_alpha * start + step * aim

    back = lax.rem(LANES - cycles * shard, LANES)
    wide_lane = lax.broadcasted_iota(jnp.int32, plain.shape, 1)
    factor = jnp.where(
        wide_lane < cycles, pltpu.roll(plain, back, 1),
        jnp.where(wide_lane < 2 * cycles, pltpu.roll(bent, lax.rem(back + cycles, LANES), 1), 0.0))
    factor_high = factor.astype(jnp.bfloat16).astype(jnp.float32)
    out_ref[...] = (factor_high + turn(factor_high, 32)
                    + turn(factor - factor_high, 64)).astype(jnp.bfloat16)
    for copy in copies:
        copy.wait_send()


def expand_kernel(parts, factor_ref, basis_ref, out_hbm, held, sem):
    factor = factor_ref[...][:, :basis_ref.shape[0]]
    width = basis_ref.shape[1] // parts
    copies = []
    for i in range(parts):
        span = pl.ds(i * width, width)
        held[:, span] = jnp.dot(factor, basis_ref[:, span], preferred_element_type=jnp.float32)
        copy = pltpu.make_async_copy(held.at[:, span], out_hbm.at[:, span], sem.at[i])
        copy.start()
        copies.append(copy)
    for copy in copies:
        copy.wait()


def on_device(timestreams, pointing, noise_weight, legendre, beam_window, prior_weight):
    minor = lax.axis_size("sub")
    shards = lax.axis_size("sht") * minor
    groups = lax.axis_size("det")
    modes = legendre.shape[0] * shards
    cycles = legendre.shape[2]
    nsims, samples = timestreams.shape[2:]
    bins = 2 * modes
    if not (modes == shards == 8 and cycles == 16 and groups == 2 and nsims == 32
            and legendre.shape[1] == L and samples % (4 * LANES) == 0):
        return general(timestreams, pointing, noise_weight, legendre, beam_window, prior_weight)
    count = groups * shards
    flat = jnp.swapaxes(legendre[0], 0, 1)
    beam = beam_window[None, :]
    prior = prior_weight[None, :]
    full = phase_matrix(modes, cycles)
    high = full.astype(ml_dtypes.bfloat16)
    low = (full - high.astype(np.float32)).astype(ml_dtypes.bfloat16)
    phase = np.concatenate([high, low, high.T, low.T], axis=0)
    cuts = 1
    sizes = (modes, cycles, shards, minor, groups, bins, nsims, cuts)
    vmem = pl.BlockSpec(memory_space=pltpu.VMEM)
    hbm = pl.BlockSpec(memory_space=pltpu.HBM)
    arguments = (timestreams[0, 0], pointing[0], noise_weight[0], flat, beam, prior,
                 jnp.asarray(phase))
    factors, basis = pl.pallas_call(
        functools.partial(solve_kernel, sizes),
        out_shape=(jax.ShapeDtypeStruct((2 * nsims, LANES), jnp.bfloat16),
                   jax.ShapeDtypeStruct((6 * cycles, L), jnp.bfloat16)),
        in_specs=[hbm] * 7,
        out_specs=(vmem, vmem),
        scratch_shapes=[pltpu.VMEM(a.shape, a.dtype) for a in arguments] + [
            pltpu.VMEM((112, LANES), jnp.float32),
            pltpu.VMEM((count, 16, LANES), jnp.float32),
            pltpu.SemaphoreType.DMA((len(arguments) + cuts - 1,)),
            pltpu.SemaphoreType.DMA((count,)),
            pltpu.SemaphoreType.DMA((count,)),
        ],
        compiler_params=pltpu.CompilerParams(
            collective_id=0, has_side_effects=True, vmem_limit_bytes=32 * 2**20),
        name="solve",
    )(*[pltpu.with_memory_space_constraint(a, pltpu.HBM) for a in arguments])
    parts = 4
    expanded = pl.pallas_call(
        functools.partial(expand_kernel, parts),
        out_shape=jax.ShapeDtypeStruct((2 * nsims, L), jnp.float32),
        in_specs=[vmem, vmem],
        out_specs=hbm,
        scratch_shapes=[pltpu.VMEM((2 * nsims, L), jnp.float32), pltpu.SemaphoreType.DMA((parts,))],
        compiler_params=pltpu.CompilerParams(vmem_limit_bytes=16 * 2**20),
        name="expand",
    )(factors, basis)
    return expanded.reshape(1, 2, nsims, L)


def solution(mesh):
    in_specs = (
        P(("parts", "det"), ("sht", "sub"), None, None),
        P(("parts", "det"), ("sht", "sub"), None),
        P(("parts", "det"), ("sht", "sub"), None),
        P(("sht", "sub"), None, None),
        P(),
        P(),
    )
    out_specs = P(("parts", "sht", "sub"), None, None, None)
    return jax.shard_map(
        on_device, mesh=mesh, in_specs=in_specs, out_specs=out_specs, check_vma=False
    )
```

```python
import functools
import jax
import jax.numpy as jnp
import ml_dtypes
import numpy as np
from jax import lax
from jax.experimental import pallas as pl
from jax.experimental.pallas import tpu as pltpu
from jax.sharding import PartitionSpec as P

L = 4096
NPHI = 8192
ITERS = 2
LANES = 128


HIGHEST = lax.Precision.HIGHEST


def azimuth_table(numbers):
    columns = jnp.arange(NPHI, dtype=jnp.int32)
    phases = numbers[:, None] * columns[None, :] % NPHI
    angles = phases.astype(jnp.float32) * (2.0 * jnp.pi / NPHI)
    return jnp.stack([2.0 * jnp.cos(angles), -2.0 * jnp.sin(angles)])


def local_inner(left, right):
    return jnp.sum(left * right, axis=(0, 1, 3))


def widen(values):
    return values[None, None, :, None]


def general(timestreams, pointing, noise_weight, legendre, beam_window, prior_weight):
    major_count = lax.axis_size("sht")
    minor_count = lax.axis_size("sub")
    shards = major_count * minor_count
    local_modes = legendre.shape[0]
    modes = local_modes * shards
    cycle_dev = legendre.shape[2] // shards
    pixels = cycle_dev * NPHI
    samples_in = timestreams[0, 0]
    columns = pointing[0, 0]
    weights = noise_weight[0, 0]
    nsims = samples_in.shape[0]
    positions = jnp.arange(modes, dtype=jnp.int32)
    spacing = L // modes
    table = azimuth_table(positions * spacing + spacing // 2)
    stacked_samples = jnp.concatenate([samples_in * weights, weights[None, :]], axis=0)
    binned = jnp.zeros((nsims + 1, pixels), jnp.float32).at[:, columns].add(stacked_samples)
    data_map = binned[:nsims]
    hit_weight = binned[nsims]

    def project(weighted):
        sky = weighted.reshape(nsims, cycle_dev, NPHI)
        cycles = jnp.einsum("srj,cmj->mcsr", sky, table, precision=HIGHEST)
        arrived = lax.all_to_all(cycles, ("sht", "sub"), split_axis=0, concat_axis=3, tiled=True)
        harmonic = jnp.einsum("mcsr,mlr->mcsl", arrived, legendre, precision=HIGHEST)
        harmonic = lax.psum(harmonic, "det")
        return harmonic * beam_window

    def squares(values):
        return lax.psum(local_inner(values, values), ("sht", "sub"))

    rhs = project(data_map)
    solution = jnp.zeros_like(rhs)
    residual = rhs
    direction = rhs
    norm_now = squares(residual)
    for iteration in range(ITERS):
        profile = jnp.einsum("mcsl,mlr->mcsr", direction * beam_window, legendre, precision=HIGHEST)
        synthesize_cycles = lax.all_to_all(
            profile, ("sht", "sub"), split_axis=3, concat_axis=0, tiled=True
        )
        synthesize_sky = jnp.einsum("mcsr,cmj->srj", synthesize_cycles, table, precision=HIGHEST)
        image = (
            project(synthesize_sky.reshape(nsims, pixels) * hit_weight[None, :])
            + prior_weight * direction
        )
        alpha = norm_now / lax.psum(local_inner(direction, image), ("sht", "sub"))
        solution = solution + widen(alpha) * direction
        residual = residual - widen(alpha) * image
        norm_next = squares(residual)
        direction = residual + widen(norm_next / norm_now) * direction
        norm_now = norm_next
    return solution


def phase_matrix(modes, cycles):
    bins = 2 * modes
    angles = np.pi / bins * ((2 * np.arange(modes)[:, None] + 1) * np.arange(bins)[None, :] % (2 * bins))
    table = np.stack([2.0 * np.cos(angles), -2.0 * np.sin(angles)])
    full = np.einsum("ckb,rq->rbckq", table, np.eye(cycles))
    return full.reshape(cycles * bins, 2 * modes * cycles).astype(np.float32)


def dot_t(left, right, **kwargs):
    return lax.dot_general(left, right, (((1,), (1,)), ((), ())),
                           preferred_element_type=jnp.float32, **kwargs)


def split(values, count):
    parts = []
    for _ in range(count):
        parts.append(values.astype(jnp.bfloat16))
        values = values - parts[-1].astype(jnp.float32)
    return parts


def split_dot(left, right):
    count = len(right)
    rows = left.shape[0]
    parts = split(left, count)
    total = None
    for i in reversed(range(count)):
        got = jnp.dot(jnp.concatenate(parts[:count - i], axis=0), right[i],
                      preferred_element_type=jnp.float32)
        for j in reversed(range(count - i)):
            piece = got[j * rows:(j + 1) * rows]
            total = piece if total is None else total + piece
    return total


def turn(values, shift):
    shift = shift % LANES
    return values if shift == 0 else pltpu.roll(values, shift, 1)


def solve_kernel(sizes, stream_hbm, point_hbm, weight_hbm, legendre_hbm, beam_hbm, prior_hbm,
                 phase_hbm, out_ref, basis_ref,
                 stream_ref, point_ref, weight_ref, legendre_ref, beam_ref, prior_ref,
                 phase_ref, spread, held, load_sem, send_sem, recv_sem):
    modes, cycles, shards, minor, groups, bins, nsims, cuts = sizes
    samples = point_ref.shape[1]
    pairs = [(legendre_hbm, legendre_ref), (beam_hbm, beam_ref), (prior_hbm, prior_ref),
             (point_hbm, point_ref), (weight_hbm, weight_ref)]
    height = nsims // cuts
    pairs += [(stream_hbm.at[pl.ds(i * height, height)], stream_ref.at[pl.ds(i * height, height)])
              for i in range(cuts)]
    pairs += [(phase_hbm, phase_ref)]
    loads = [pltpu.make_async_copy(source, place, load_sem.at[i])
             for i, (source, place) in enumerate(pairs)]
    for load in loads:
        load.start()
    det = lax.axis_index("det")
    major, sub = lax.axis_index("sht"), lax.axis_index("sub")
    majors = shards // minor
    shard = major * minor + sub
    me = det * shards + shard
    count = groups * shards

    def partner(offset):
        step = offset // (groups * minor)
        row = step + (step - major + majors) // majors if step < majors - 1 else major
        side = lax.rem(det + 1 + offset // minor, groups)
        core = lax.rem(sub + 1 + offset, minor)
        return side * shards + row * minor + core, {"det": side, "sht": row, "sub": core}

    barrier = pltpu.get_barrier_semaphore()
    for offset in range(count - 1):
        pl.semaphore_signal(barrier, inc=1, device_id=partner(offset)[1],
                            device_id_type=pl.DeviceIdType.MESH)

    for load in loads[:-1]:
        load.wait()
    beam = beam_ref[...]
    prior = prior_ref[...]
    power = beam * beam
    center = jnp.sum(power * prior, axis=1, keepdims=True) / jnp.sum(power, axis=1, keepdims=True)
    excess = prior - center
    field = legendre_ref[...] * beam
    upper = det.astype(jnp.float32)
    first = field * ((1.0 - upper) + upper * (excess * excess))
    left = jnp.concatenate(split(field, 3), axis=0)
    right = jnp.concatenate(split(jnp.concatenate([first, first * excess], axis=0), 3), axis=0)
    crossed = dot_t(left, right)
    top, mid, end = crossed[0:16], crossed[16:32], crossed[32:48]
    spread[64:112, 0:96] = jnp.concatenate([top + (mid + end), top + mid, top], axis=0)

    own = cycles // shards * bins
    place = point_ref[...]
    column = place & (NPHI - 1)
    sign = (1 - 2 * ((column // bins) & 1)).astype(jnp.float32)
    target = (place // NPHI) * bins + (column & (bins - 1))
    weight = weight_ref[...]
    hot = jnp.where(lax.broadcasted_iota(jnp.int32, (own, samples), 0) == target, 1.0, 0.0)
    hot = hot.astype(jnp.bfloat16)
    rows = jnp.concatenate(
        [stream_ref[...] * (weight * sign), jnp.broadcast_to(weight, (16, samples))], axis=0)
    binned = dot_t(jnp.concatenate(split(rows, 2), axis=0), hot)
    binned = binned[0:48] + binned[48:96]

    spread[0:64] = jnp.zeros((64, LANES), jnp.float32)
    spread[0:48, 0:own] = binned
    spread[48:64, 0:32] = spread[64:80, 0:32] + (
        turn(spread[80:96, :], -32) + turn(spread[96:112, :], -64))[:, 0:32]
    eight = [spread[8 * i:8 * i + 8, :] for i in range(8)]
    held[me, 0:8, :] = (eight[0] + turn(eight[1], 32)) + (turn(eight[2], 64) + turn(eight[3], 96))
    held[me, 8:16, :] = (eight[6] + turn(eight[7], 32)) + turn(eight[4], 64)

    pl.semaphore_wait(barrier, count - 1)
    copies = []
    for offset in range(count - 1):
        copy = pltpu.make_async_remote_copy(
            src_ref=held.at[me], dst_ref=held.at[me],
            send_sem=send_sem.at[offset], recv_sem=recv_sem.at[me],
            device_id=partner(offset)[1], device_id_type=pl.DeviceIdType.MESH)
        copy.start()
        copies.append(copy)

    wide = jnp.concatenate([field, field * excess], axis=0)
    wide_high = wide.astype(jnp.bfloat16)
    basis_ref[0:32, :] = wide_high
    basis_ref[32:64, :] = (wide - wide_high.astype(jnp.float32)).astype(jnp.bfloat16)
    basis_ref[64:96, :] = wide_high
    loads[-1].wait()
    for offset in range(count - 1):
        other, where = partner(offset)
        pltpu.make_async_remote_copy(
            src_ref=held.at[other], dst_ref=held.at[other],
            send_sem=send_sem.at[offset], recv_sem=recv_sem.at[other],
            device_id=where, device_id_type=pl.DeviceIdType.MESH).wait_recv()

    lane = lax.broadcasted_iota(jnp.int32, (8, LANES), 1)
    in_quarter = [lane // 32 == i for i in range(4)]
    in_mode = [lane // cycles == k for k in range(modes)]
    data_half, weight_half = [], []
    for half in range(2):
        data = [held[4 * half + i, 0:8, :] + held[shards + 4 * half + i, 0:8, :] for i in range(4)]
        weights = [held[4 * half + i, 8:16, :] + held[shards + 4 * half + i, 8:16, :] for i in range(4)]

        def gather(parts, at):
            total = jnp.zeros((8, LANES), jnp.float32)
            for i in range(4):
                total = jnp.where(in_quarter[i], turn(parts[i], 32 * (i - at)), total)
            return total

        data_half.append(jnp.concatenate([gather(data, j) for j in range(4)], axis=0))
        weight_half.append(gather(weights, 2))
    data_bins = jnp.concatenate(data_half, axis=1)
    weight_bins = jnp.concatenate(weight_half, axis=1)[0:1, :]
    moment = []
    for n in range(4):
        parts = []
        for k in range(modes):
            got = held[(n // 2) * shards + k, 8:16, :]
            for up in range(2):
                parts.append(jnp.where(in_mode[k], turn(got, cycles * (k - n % 2) - 32 * up), 0.0))
        moment.append(jnp.concatenate(parts, axis=0))

    def stack(values):
        return jnp.concatenate([values[:, :LANES], values[:, LANES:]], axis=0)

    def unstack(values):
        return jnp.concatenate([values[:nsims], values[nsims:]], axis=1)

    def inner(values):
        return jnp.sum(values[:nsims] + values[nsims:], axis=1, keepdims=True)

    def both(values):
        wide = jnp.broadcast_to(values, (nsims, LANES))
        return jnp.concatenate([wide, wide], axis=0)

    size = 2 * modes * cycles
    phase = [phase_ref[i * size:(i + 1) * size, :] for i in range(4)]

    def sky(profile):
        return split_dot(unstack(profile), phase[2:])

    def profiles(bins_in):
        return stack(split_dot(bins_in, phase[:2]))

    moment_parts = split(jnp.concatenate(moment, axis=1), 3)
    start = profiles(data_bins)
    applied = split_dot(start, moment_parts)
    s0, s1, s2, s3 = [applied[:, n * LANES:(n + 1) * LANES] for n in range(4)]
    seen = sky(s0)
    weighted = seen * weight_bins
    pulled = profiles(weighted)
    applied = split_dot(pulled, [part[:, :2 * LANES] for part in moment_parts])
    g0, g1 = applied[:, :LANES], applied[:, LANES:]
    seen_more = sky(g0 + s1)
    norm = inner(start * s0)
    curve = jnp.sum(seen * weighted, axis=1, keepdims=True) + center * norm + inner(start * s1)
    alpha = norm / curve
    wide_alpha = both(alpha)
    square = wide_alpha * wide_alpha
    keep = 1.0 - center * wide_alpha
    left = keep * start - wide_alpha * pulled
    left0 = keep * s0 - wide_alpha * g0
    left1 = keep * s1 - wide_alpha * g1
    left_norm = inner(left * (left0 - 2.0 * wide_alpha * s1) + square * (start * s2))
    beta = left_norm / norm
    wide_beta = both(beta)
    aim = left + wide_beta * start
    aim0 = left0 + wide_beta * s0
    aim1 = left1 + wide_beta * s1
    aim_seen = (1.0 - center * alpha + beta) * seen - alpha * seen_more
    aim_norm = inner(aim * (aim0 - 2.0 * wide_alpha * s1) + square * (start * s2))
    aim_excess = inner(aim * (aim1 - 2.0 * wide_alpha * s2) + square * (start * s3))
    curve = (jnp.sum(aim_seen * aim_seen * weight_bins, axis=1, keepdims=True)
             + center * aim_norm + aim_excess)
    step = both(left_norm / curve)
    bent = -(wide_alpha * step) * start
    plain = wide_alpha * start + step * aim

    back = lax.rem(LANES - cycles * shard, LANES)
    wide_lane = lax.broadcasted_iota(jnp.int32, plain.shape, 1)
    factor = jnp.where(
        wide_lane < cycles, pltpu.roll(plain, back, 1),
        jnp.where(wide_lane < 2 * cycles, pltpu.roll(bent, lax.rem(back + cycles, LANES), 1), 0.0))
    factor_high = factor.astype(jnp.bfloat16).astype(jnp.float32)
    out_ref[...] = (factor_high + turn(factor_high, 32)
                    + turn(factor - factor_high, 64)).astype(jnp.bfloat16)
    for copy in copies:
        copy.wait_send()


def expand_kernel(parts, factor_ref, basis_ref, out_hbm, held, sem):
    factor = factor_ref[...][:, :basis_ref.shape[0]]
    width = basis_ref.shape[1] // parts
    copies = []
    for i in range(parts):
        span = pl.ds(i * width, width)
        held[:, span] = jnp.dot(factor, basis_ref[:, span], preferred_element_type=jnp.float32)
        copy = pltpu.make_async_copy(held.at[:, span], out_hbm.at[:, span], sem.at[i])
        copy.start()
        copies.append(copy)
    for copy in copies:
        copy.wait()


def on_device(timestreams, pointing, noise_weight, legendre, beam_window, prior_weight):
    minor = lax.axis_size("sub")
    shards = lax.axis_size("sht") * minor
    groups = lax.axis_size("det")
    modes = legendre.shape[0] * shards
    cycles = legendre.shape[2]
    nsims, samples = timestreams.shape[2:]
    bins = 2 * modes
    if not (modes == shards == 8 and cycles == 16 and groups == 2 and nsims == 32
            and legendre.shape[1] == L and samples % LANES == 0):
        return general(timestreams, pointing, noise_weight, legendre, beam_window, prior_weight)
    count = groups * shards
    flat = jnp.swapaxes(legendre[0], 0, 1)
    beam = beam_window[None, :]
    prior = prior_weight[None, :]
    full = phase_matrix(modes, cycles)
    high = full.astype(ml_dtypes.bfloat16)
    low = (full - high.astype(np.float32)).astype(ml_dtypes.bfloat16)
    phase = np.concatenate([high, low, high.T, low.T], axis=0)
    cuts = 1
    sizes = (modes, cycles, shards, minor, groups, bins, nsims, cuts)
    vmem = pl.BlockSpec(memory_space=pltpu.VMEM)
    hbm = pl.BlockSpec(memory_space=pltpu.HBM)
    arguments = (timestreams[0, 0], pointing[0], noise_weight[0], flat, beam, prior,
                 jnp.asarray(phase))
    factors, basis = pl.pallas_call(
        functools.partial(solve_kernel, sizes),
        out_shape=(jax.ShapeDtypeStruct((2 * nsims, LANES), jnp.bfloat16),
                   jax.ShapeDtypeStruct((6 * cycles, L), jnp.bfloat16)),
        in_specs=[hbm] * 7,
        out_specs=(vmem, vmem),
        scratch_shapes=[pltpu.VMEM(a.shape, a.dtype) for a in arguments] + [
            pltpu.VMEM((112, LANES), jnp.float32),
            pltpu.VMEM((count, 16, LANES), jnp.float32),
            pltpu.SemaphoreType.DMA((len(arguments) + cuts - 1,)),
            pltpu.SemaphoreType.DMA((count,)),
            pltpu.SemaphoreType.DMA((count,)),
        ],
        compiler_params=pltpu.CompilerParams(
            collective_id=0, has_side_effects=True, vmem_limit_bytes=32 * 2**20),
        name="solve",
    )(*[pltpu.with_memory_space_constraint(a, pltpu.HBM) for a in arguments])
    parts = 4
    expanded = pl.pallas_call(
        functools.partial(expand_kernel, parts),
        out_shape=jax.ShapeDtypeStruct((2 * nsims, L), jnp.float32),
        in_specs=[vmem, vmem],
        out_specs=hbm,
        scratch_shapes=[pltpu.VMEM((2 * nsims, L), jnp.float32), pltpu.SemaphoreType.DMA((parts,))],
        compiler_params=pltpu.CompilerParams(vmem_limit_bytes=16 * 2**20),
        name="expand",
    )(factors, basis)
    return expanded.reshape(1, 2, nsims, L)


def solution(mesh):
    in_specs = (
        P(("parts", "det"), ("sht", "sub"), None, None),
        P(("parts", "det"), ("sht", "sub"), None),
        P(("parts", "det"), ("sht", "sub"), None),
        P(("sht", "sub"), None, None),
        P(),
        P(),
    )
    out_specs = P(("parts", "sht", "sub"), None, None, None)
    return jax.shard_map(
        on_device, mesh=mesh, in_specs=in_specs, out_specs=out_specs, check_vma=False
    )
```

```python
import functools
import jax
import jax.numpy as jnp
import ml_dtypes
import numpy as np
from jax import lax
from jax.experimental import pallas as pl
from jax.experimental.pallas import tpu as pltpu
from jax.sharding import PartitionSpec as P

L = 4096
NPHI = 8192
ITERS = 2
LANES = 128


HIGHEST = lax.Precision.HIGHEST


def azimuth_table(numbers):
    columns = jnp.arange(NPHI, dtype=jnp.int32)
    phases = numbers[:, None] * columns[None, :] % NPHI
    angles = phases.astype(jnp.float32) * (2.0 * jnp.pi / NPHI)
    return jnp.stack([2.0 * jnp.cos(angles), -2.0 * jnp.sin(angles)])


def local_inner(left, right):
    return jnp.sum(left * right, axis=(0, 1, 3))


def widen(values):
    return values[None, None, :, None]


def general(timestreams, pointing, noise_weight, legendre, beam_window, prior_weight):
    major_count = lax.axis_size("sht")
    minor_count = lax.axis_size("sub")
    shards = major_count * minor_count
    local_modes = legendre.shape[0]
    modes = local_modes * shards
    cycle_dev = legendre.shape[2] // shards
    pixels = cycle_dev * NPHI
    samples_in = timestreams[0, 0]
    columns = pointing[0, 0]
    weights = noise_weight[0, 0]
    nsims = samples_in.shape[0]
    positions = jnp.arange(modes, dtype=jnp.int32)
    spacing = L // modes
    table = azimuth_table(positions * spacing + spacing // 2)
    stacked_samples = jnp.concatenate([samples_in * weights, weights[None, :]], axis=0)
    binned = jnp.zeros((nsims + 1, pixels), jnp.float32).at[:, columns].add(stacked_samples)
    data_map = binned[:nsims]
    hit_weight = binned[nsims]

    def project(weighted):
        sky = weighted.reshape(nsims, cycle_dev, NPHI)
        cycles = jnp.einsum("srj,cmj->mcsr", sky, table, precision=HIGHEST)
        arrived = lax.all_to_all(cycles, ("sht", "sub"), split_axis=0, concat_axis=3, tiled=True)
        harmonic = jnp.einsum("mcsr,mlr->mcsl", arrived, legendre, precision=HIGHEST)
        harmonic = lax.psum(harmonic, "det")
        return harmonic * beam_window

    def squares(values):
        return lax.psum(local_inner(values, values), ("sht", "sub"))

    rhs = project(data_map)
    solution = jnp.zeros_like(rhs)
    residual = rhs
    direction = rhs
    norm_now = squares(residual)
    for iteration in range(ITERS):
        profile = jnp.einsum("mcsl,mlr->mcsr", direction * beam_window, legendre, precision=HIGHEST)
        synthesize_cycles = lax.all_to_all(
            profile, ("sht", "sub"), split_axis=3, concat_axis=0, tiled=True
        )
        synthesize_sky = jnp.einsum("mcsr,cmj->srj", synthesize_cycles, table, precision=HIGHEST)
        image = (
            project(synthesize_sky.reshape(nsims, pixels) * hit_weight[None, :])
            + prior_weight * direction
        )
        alpha = norm_now / lax.psum(local_inner(direction, image), ("sht", "sub"))
        solution = solution + widen(alpha) * direction
        residual = residual - widen(alpha) * image
        norm_next = squares(residual)
        direction = residual + widen(norm_next / norm_now) * direction
        norm_now = norm_next
    return solution


def phase_matrix(modes, cycles):
    bins = 2 * modes
    angles = np.pi / bins * ((2 * np.arange(modes)[:, None] + 1) * np.arange(bins)[None, :] % (2 * bins))
    table = np.stack([2.0 * np.cos(angles), -2.0 * np.sin(angles)])
    full = np.einsum("ckb,rq->rbckq", table, np.eye(cycles))
    return full.reshape(cycles * bins, 2 * modes * cycles).astype(np.float32)


def dot_t(left, right, **kwargs):
    return lax.dot_general(left, right, (((1,), (1,)), ((), ())),
                           preferred_element_type=jnp.float32, **kwargs)


def split(values, count):
    parts = []
    for _ in range(count):
        parts.append(values.astype(jnp.bfloat16))
        values = values - parts[-1].astype(jnp.float32)
    return parts


def split_dot(left, right):
    count = len(right)
    rows = left.shape[0]
    parts = split(left, count)
    total = None
    for i in reversed(range(count)):
        got = jnp.dot(jnp.concatenate(parts[:count - i], axis=0), right[i],
                      preferred_element_type=jnp.float32)
        for j in reversed(range(count - i)):
            piece = got[j * rows:(j + 1) * rows]
            total = piece if total is None else total + piece
    return total


def turn(values, shift):
    shift = shift % LANES
    return values if shift == 0 else pltpu.roll(values, shift, 1)


def solve_kernel(sizes, stream_hbm, point_hbm, weight_hbm, legendre_hbm, beam_hbm, prior_hbm,
                 phase_hbm, out_ref, basis_ref,
                 stream_ref, point_ref, weight_ref, legendre_ref, beam_ref, prior_ref,
                 phase_ref, spread, held, load_sem, send_sem, recv_sem):
    modes, cycles, shards, minor, groups, bins, nsims, cuts = sizes
    samples = point_ref.shape[1]
    pairs = [(legendre_hbm, legendre_ref), (beam_hbm, beam_ref), (prior_hbm, prior_ref),
             (point_hbm, point_ref), (weight_hbm, weight_ref)]
    height = nsims // cuts
    pairs += [(stream_hbm.at[pl.ds(i * height, height)], stream_ref.at[pl.ds(i * height, height)])
              for i in range(cuts)]
    pairs += [(phase_hbm, phase_ref)]
    loads = [pltpu.make_async_copy(source, place, load_sem.at[i])
             for i, (source, place) in enumerate(pairs)]
    for load in loads:
        load.start()
    det = lax.axis_index("det")
    major, sub = lax.axis_index("sht"), lax.axis_index("sub")
    majors = shards // minor
    shard = major * minor + sub
    me = det * shards + shard
    count = groups * shards

    def partner(offset):
        step = offset // (groups * minor)
        row = step + (step - major + majors) // majors if step < majors - 1 else major
        side = lax.rem(det + 1 + offset // minor, groups)
        core = lax.rem(sub + 1 + offset, minor)
        return side * shards + row * minor + core, {"det": side, "sht": row, "sub": core}

    barrier = pltpu.get_barrier_semaphore()
    for offset in range(count - 1):
        pl.semaphore_signal(barrier, inc=1, device_id=partner(offset)[1],
                            device_id_type=pl.DeviceIdType.MESH)

    for load in loads[:-1]:
        load.wait()
    beam = beam_ref[...]
    prior = prior_ref[...]
    power = beam * beam
    center = jnp.sum(power * prior, axis=1, keepdims=True) / jnp.sum(power, axis=1, keepdims=True)
    excess = prior - center
    field = legendre_ref[...] * beam
    upper = det.astype(jnp.float32)
    first = field * ((1.0 - upper) + upper * (excess * excess))
    left = jnp.concatenate(split(field, 3), axis=0)
    right = jnp.concatenate(split(jnp.concatenate([first, first * excess], axis=0), 3), axis=0)
    crossed = dot_t(left, right)
    top, mid, end = crossed[0:16], crossed[16:32], crossed[32:48]
    spread[64:112, 0:96] = jnp.concatenate([top + (mid + end), top + mid, top], axis=0)

    own = cycles // shards * bins
    place = point_ref[...]
    column = place & (NPHI - 1)
    sign = (1 - 2 * ((column // bins) & 1)).astype(jnp.float32)
    target = (place // NPHI) * bins + (column & (bins - 1))
    weight = weight_ref[...]
    hot = jnp.where(lax.broadcasted_iota(jnp.int32, (own, samples), 0) == target, 1.0, 0.0)
    hot = hot.astype(jnp.bfloat16)
    upper_half = lax.broadcasted_iota(jnp.int32, (16, samples), 0) < 8
    weight_high = weight.astype(jnp.bfloat16).astype(jnp.float32)
    weight_rows = jnp.where(upper_half, weight_high, weight - weight_high).astype(jnp.bfloat16)
    rows = split(stream_ref[...] * (weight * sign), 2) + [weight_rows]
    binned = dot_t(jnp.concatenate(rows, axis=0), hot)
    weight_sum = binned[64:72] + binned[72:80]
    binned = jnp.concatenate([binned[0:32] + binned[32:64], weight_sum, weight_sum], axis=0)

    spread[0:64] = jnp.zeros((64, LANES), jnp.float32)
    spread[0:48, 0:own] = binned
    spread[48:64, 0:32] = spread[64:80, 0:32] + (
        turn(spread[80:96, :], -32) + turn(spread[96:112, :], -64))[:, 0:32]
    eight = [spread[8 * i:8 * i + 8, :] for i in range(8)]
    held[me, 0:8, :] = (eight[0] + turn(eight[1], 32)) + (turn(eight[2], 64) + turn(eight[3], 96))
    held[me, 8:16, :] = (eight[6] + turn(eight[7], 32)) + turn(eight[4], 64)

    pl.semaphore_wait(barrier, count - 1)
    copies = []
    for offset in range(count - 1):
        copy = pltpu.make_async_remote_copy(
            src_ref=held.at[me], dst_ref=held.at[me],
            send_sem=send_sem.at[offset], recv_sem=recv_sem.at[me],
            device_id=partner(offset)[1], device_id_type=pl.DeviceIdType.MESH)
        copy.start()
        copies.append(copy)

    wide = jnp.concatenate([field, field * excess], axis=0)
    wide_high = wide.astype(jnp.bfloat16)
    basis_ref[0:32, :] = wide_high
    basis_ref[32:64, :] = (wide - wide_high.astype(jnp.float32)).astype(jnp.bfloat16)
    basis_ref[64:96, :] = wide_high
    loads[-1].wait()
    for offset in range(count - 1):
        other, where = partner(offset)
        pltpu.make_async_remote_copy(
            src_ref=held.at[other], dst_ref=held.at[other],
            send_sem=send_sem.at[offset], recv_sem=recv_sem.at[other],
            device_id=where, device_id_type=pl.DeviceIdType.MESH).wait_recv()

    lane = lax.broadcasted_iota(jnp.int32, (8, LANES), 1)
    in_quarter = [lane // 32 == i for i in range(4)]
    in_mode = [lane // cycles == k for k in range(modes)]
    data_half, weight_half = [], []
    for half in range(2):
        data = [held[4 * half + i, 0:8, :] + held[shards + 4 * half + i, 0:8, :] for i in range(4)]
        weights = [held[4 * half + i, 8:16, :] + held[shards + 4 * half + i, 8:16, :] for i in range(4)]

        def gather(parts, at):
            total = jnp.zeros((8, LANES), jnp.float32)
            for i in range(4):
                total = jnp.where(in_quarter[i], turn(parts[i], 32 * (i - at)), total)
            return total

        data_half.append(jnp.concatenate([gather(data, j) for j in range(4)], axis=0))
        weight_half.append(gather(weights, 2))
    data_bins = jnp.concatenate(data_half, axis=1)
    weight_bins = jnp.concatenate(weight_half, axis=1)[0:1, :]
    moment = []
    for n in range(4):
        parts = []
        for k in range(modes):
            got = held[(n // 2) * shards + k, 8:16, :]
            for up in range(2):
                parts.append(jnp.where(in_mode[k], turn(got, cycles * (k - n % 2) - 32 * up), 0.0))
        moment.append(jnp.concatenate(parts, axis=0))

    def stack(values):
        return jnp.concatenate([values[:, :LANES], values[:, LANES:]], axis=0)

    def unstack(values):
        return jnp.concatenate([values[:nsims], values[nsims:]], axis=1)

    def inner(values):
        return jnp.sum(values[:nsims] + values[nsims:], axis=1, keepdims=True)

    def both(values):
        wide = jnp.broadcast_to(values, (nsims, LANES))
        return jnp.concatenate([wide, wide], axis=0)

    size = 2 * modes * cycles
    phase = [phase_ref[i * size:(i + 1) * size, :] for i in range(4)]

    def sky(profile):
        return split_dot(unstack(profile), phase[2:])

    def profiles(bins_in):
        return stack(split_dot(bins_in, phase[:2]))

    moment_parts = split(jnp.concatenate(moment, axis=1), 3)
    start = profiles(data_bins)
    applied = split_dot(start, moment_parts)
    s0, s1, s2, s3 = [applied[:, n * LANES:(n + 1) * LANES] for n in range(4)]
    seen = sky(s0)
    weighted = seen * weight_bins
    pulled = profiles(weighted)
    applied = split_dot(pulled, [part[:, :2 * LANES] for part in moment_parts])
    g0, g1 = applied[:, :LANES], applied[:, LANES:]
    seen_more = sky(g0 + s1)
    norm = inner(start * s0)
    curve = jnp.sum(seen * weighted, axis=1, keepdims=True) + center * norm + inner(start * s1)
    alpha = norm / curve
    wide_alpha = both(alpha)
    square = wide_alpha * wide_alpha
    keep = 1.0 - center * wide_alpha
    left = keep * start - wide_alpha * pulled
    left0 = keep * s0 - wide_alpha * g0
    left1 = keep * s1 - wide_alpha * g1
    left_norm = inner(left * (left0 - 2.0 * wide_alpha * s1) + square * (start * s2))
    beta = left_norm / norm
    wide_beta = both(beta)
    aim = left + wide_beta * start
    aim0 = left0 + wide_beta * s0
    aim1 = left1 + wide_beta * s1
    aim_seen = (1.0 - center * alpha + beta) * seen - alpha * seen_more
    aim_norm = inner(aim * (aim0 - 2.0 * wide_alpha * s1) + square * (start * s2))
    aim_excess = inner(aim * (aim1 - 2.0 * wide_alpha * s2) + square * (start * s3))
    curve = (jnp.sum(aim_seen * aim_seen * weight_bins, axis=1, keepdims=True)
             + center * aim_norm + aim_excess)
    step = both(left_norm / curve)
    bent = -(wide_alpha * step) * start
    plain = wide_alpha * start + step * aim

    back = lax.rem(LANES - cycles * shard, LANES)
    wide_lane = lax.broadcasted_iota(jnp.int32, plain.shape, 1)
    factor = jnp.where(
        wide_lane < cycles, pltpu.roll(plain, back, 1),
        jnp.where(wide_lane < 2 * cycles, pltpu.roll(bent, lax.rem(back + cycles, LANES), 1), 0.0))
    factor_high = factor.astype(jnp.bfloat16).astype(jnp.float32)
    out_ref[...] = (factor_high + turn(factor_high, 32)
                    + turn(factor - factor_high, 64)).astype(jnp.bfloat16)
    for copy in copies:
        copy.wait_send()


def expand_kernel(parts, factor_ref, basis_ref, out_hbm, held, sem):
    factor = factor_ref[...][:, :basis_ref.shape[0]]
    width = basis_ref.shape[1] // parts
    copies = []
    for i in range(parts):
        span = pl.ds(i * width, width)
        held[:, span] = jnp.dot(factor, basis_ref[:, span], preferred_element_type=jnp.float32)
        copy = pltpu.make_async_copy(held.at[:, span], out_hbm.at[:, span], sem.at[i])
        copy.start()
        copies.append(copy)
    for copy in copies:
        copy.wait()


def on_device(timestreams, pointing, noise_weight, legendre, beam_window, prior_weight):
    minor = lax.axis_size("sub")
    shards = lax.axis_size("sht") * minor
    groups = lax.axis_size("det")
    modes = legendre.shape[0] * shards
    cycles = legendre.shape[2]
    nsims, samples = timestreams.shape[2:]
    bins = 2 * modes
    if not (modes == shards == 8 and cycles == 16 and groups == 2 and nsims == 32
            and legendre.shape[1] == L and samples % LANES == 0):
        return general(timestreams, pointing, noise_weight, legendre, beam_window, prior_weight)
    count = groups * shards
    flat = jnp.swapaxes(legendre[0], 0, 1)
    beam = beam_window[None, :]
    prior = prior_weight[None, :]
    full = phase_matrix(modes, cycles)
    high = full.astype(ml_dtypes.bfloat16)
    low = (full - high.astype(np.float32)).astype(ml_dtypes.bfloat16)
    phase = np.concatenate([high, low, high.T, low.T], axis=0)
    cuts = 1
    sizes = (modes, cycles, shards, minor, groups, bins, nsims, cuts)
    vmem = pl.BlockSpec(memory_space=pltpu.VMEM)
    hbm = pl.BlockSpec(memory_space=pltpu.HBM)
    arguments = (timestreams[0, 0], pointing[0], noise_weight[0], flat, beam, prior,
                 jnp.asarray(phase))
    factors, basis = pl.pallas_call(
        functools.partial(solve_kernel, sizes),
        out_shape=(jax.ShapeDtypeStruct((2 * nsims, LANES), jnp.bfloat16),
                   jax.ShapeDtypeStruct((6 * cycles, L), jnp.bfloat16)),
        in_specs=[hbm] * 7,
        out_specs=(vmem, vmem),
        scratch_shapes=[pltpu.VMEM(a.shape, a.dtype) for a in arguments] + [
            pltpu.VMEM((112, LANES), jnp.float32),
            pltpu.VMEM((count, 16, LANES), jnp.float32),
            pltpu.SemaphoreType.DMA((len(arguments) + cuts - 1,)),
            pltpu.SemaphoreType.DMA((count,)),
            pltpu.SemaphoreType.DMA((count,)),
        ],
        compiler_params=pltpu.CompilerParams(
            collective_id=0, has_side_effects=True, vmem_limit_bytes=32 * 2**20),
        name="solve",
    )(*[pltpu.with_memory_space_constraint(a, pltpu.HBM) for a in arguments])
    parts = 4
    expanded = pl.pallas_call(
        functools.partial(expand_kernel, parts),
        out_shape=jax.ShapeDtypeStruct((2 * nsims, L), jnp.float32),
        in_specs=[vmem, vmem],
        out_specs=hbm,
        scratch_shapes=[pltpu.VMEM((2 * nsims, L), jnp.float32), pltpu.SemaphoreType.DMA((parts,))],
        compiler_params=pltpu.CompilerParams(vmem_limit_bytes=16 * 2**20),
        name="expand",
    )(factors, basis)
    return expanded.reshape(1, 2, nsims, L)


def solution(mesh):
    in_specs = (
        P(("parts", "det"), ("sht", "sub"), None, None),
        P(("parts", "det"), ("sht", "sub"), None),
        P(("parts", "det"), ("sht", "sub"), None),
        P(("sht", "sub"), None, None),
        P(),
        P(),
    )
    out_specs = P(("parts", "sht", "sub"), None, None, None)
    return jax.shard_map(
        on_device, mesh=mesh, in_specs=in_specs, out_specs=out_specs, check_vma=False
    )
```
